32 devices in a mesh: parts: 2 (over y), row: 4 (over z), col: 4 (over x, core).
Axes of the slice: x: 2, y: 2, z: 4, core: 2. Of those that a mesh axis runs over, the one named last changes fastest.
Arguments:
- wavefunction: bfloat16 [128, 128, 128], P('parts', 'col'), parts along dimension 0, may hold values from -6 to 6
- left_ops: bfloat16 [768, 128, 128], P(('parts', 'row')), parts along dimension 0, may hold values from -0.5 to 0.5
- right_ops: bfloat16 [768, 128, 128], P(('parts', 'row'), 'col'), parts along dimension 0, may hold values from -0.0625 to 0.0625
- term_source: int32 [768], P(('parts', 'row')), parts along dimension 0, may hold values from 0 to 63
- term_target: int32 [768], P(('parts', 'row')), parts along dimension 0, may hold values from 0 to 63
- term_count: int32 [8], P(('parts', 'row')), parts along dimension 0, may hold values from 1 to 96, 240 in all
- left_dims: int32 [128], P('parts'), parts along dimension 0, may hold values from 1 to 128, 6144 in all
- right_dims: int32 [128], P('parts'), parts along dimension 0, may hold values from 1 to 128, 5120 in all
Outputs:
- sigmas: float32 [3, 128, 128, 128], P(None, ('parts', 'row'), 'col'), parts along dimension 1
The draws below stay inside these ranges and needn't reach their ends.
There are 2 independent parts, one for each index of `parts`. The reference program is written for one: setup_inputs(seed, part) draws one part's arguments, and reference() takes and returns one part's arrays. A program takes and returns all parts, laid end to end along the dimension named above; each array names one. Nothing has to cross between parts.
Inputs may be any that keep to these rules, and one draw needn't show every extreme that they name: The busiest index of row has exactly 96 live slots; slots from term_count on are unused. `left_dims`: the largest equals 128. `right_dims`: the largest equals 128.
All inputs are finite; a program needn't handle non-finite values. No bound on the sum of `term_count` on one device may be relied on, other than what follows from the above.
Results may differ from the reference program's by a relative error of at most 0.0032.
Values may be sent and summed in bfloat16 or wider, within the bound.
A program may use at most 64 MiB of HBM per device.

```python
import math
import jax
import jax.numpy as jnp
import numpy as np
from jax import lax

S = 64
B = 128
W = 128
P_DEV = 96
TERMS = 384
STEPS = 3
N_ROW = 4


def set_ends(array, key, least, largest):
    place = [jax.random.randint(jax.random.fold_in(key, axis), (), 0, length) for axis, length in enumerate(array.shape)]
    longest = array.shape.index(max(array.shape))
    beside = place[:longest] + [(place[longest] + 1) % array.shape[longest]] + place[longest + 1:]
    return array.at[tuple(place)].set(least).at[tuple(beside)].set(largest)


def shard_levels(key, shape, shards, smallest, largest):
    factor_of = 1.0
    for position, parts in shards:
        heights = jax.random.uniform(jax.random.fold_in(jax.random.fold_in(key, 6), position), (parts,), jnp.float32, smallest / len(shards), largest / len(shards))
        factor_of = factor_of * jnp.repeat(jnp.exp(heights), shape[position] // parts).reshape((-1,) + (1,) * (len(shape) - 1 - position))
    return factor_of


def rank_table(count, slope):
    weights = [(1 << 20) // math.isqrt(rank ** slope) + 1 for rank in range(1, count + 1)]
    scale = 1 + sum(weights) // (1 << 30)
    return np.cumsum(np.array([max(1, weight // scale) for weight in weights]))


def ranked_ids(stream_key, dims, number_of, skew):
    grid = rank_table(number_of, skew)
    pick = jax.random.randint(jax.random.fold_in(stream_key, 1), dims, 0, int(grid[number_of - 1]))
    rank = jnp.searchsorted(jnp.asarray(grid, jnp.int32), pick, side="right")
    return jax.random.permutation(jax.random.fold_in(stream_key, 2), number_of)[rank].astype(jnp.int32)


def length_profile(count, total, most, lean):
    weights = [(1 << 20) // math.isqrt(grade ** lean) + 1 for grade in range(2, count + 1)]
    surplus, given = total - most - (count - 1), [1] * (count - 1)
    while surplus > 0:
        movable = [i for i in range(count - 1) if given[i] < most]
        mass, budget = sum([weights[i] for i in movable]), surplus
        for i in movable:
            extra = min(most - given[i], max(1, budget * weights[i] // mass), surplus)
            given[i] = given[i] + extra
            surplus = surplus - extra
    return np.array([most] + given)


def ragged_sizes(own_key, amount, total, limit, slope):
    if amount == 2:
        one = jax.random.randint(own_key, (), max(1, total - limit), min(limit, total - 1) + 1)
        return jnp.stack([one, total - one])
    sizes = jnp.asarray(length_profile(amount, total, limit, slope), jnp.int32)
    couples = (amount - 1) // 2
    source_of, sink = sizes[1:1 + 2 * couples:2], sizes[2:2 + 2 * couples:2]
    slack = jnp.minimum(source_of - 1, limit - sink)
    moved = jax.random.randint(jax.random.fold_in(own_key, 1), (couples,), 0, 1 << 20) % (slack + 1)
    sizes = sizes.at[1:1 + 2 * couples:2].set(source_of - moved).at[2:2 + 2 * couples:2].set(sink + moved)
    return sizes[jax.random.permutation(jax.random.fold_in(own_key, 2), amount)]


def centred(stream_key, shape, width, bound, cuts=(), kind=jnp.bfloat16):
    result = jax.random.normal(stream_key, shape, jnp.float32) * width
    if len(cuts) > 0:
        result = shard_levels(stream_key, shape, cuts, -0.22, 0.18) * result
    return jnp.clip(result, min=-bound, max=bound).astype(kind)


def setup_inputs(seed: int = 0, part: int = 0) -> dict:
    key_list = jax.random.split(jax.random.key(seed), 9)
    part_keys = jax.random.split(jax.random.fold_in(key_list[8], part), 9)
    return {
        "wavefunction": centred(part_keys[0], (S, W, B), 1.0, 6.0, ((1, 4),)),
        "left_ops": centred(part_keys[1], (TERMS, B, B), B ** -0.5, 0.5, ((0, 4),)),
        "right_ops": centred(part_keys[2], (TERMS, W, W), (W * 64) ** -0.5, 0.0625, ((0, 4), (1, 4))),
        "term_source": set_ends(jax.random.randint(part_keys[3], (TERMS,), 0, S), jax.random.fold_in(part_keys[3], 1), 0, S - 1).astype(jnp.int32),
        "term_target": set_ends(ranked_ids(part_keys[4], (TERMS,), S, 1), jax.random.fold_in(part_keys[4], 3), 0, S - 1).astype(jnp.int32),
        "term_count": ragged_sizes(part_keys[5], N_ROW, N_ROW * P_DEV * 5 // 8, P_DEV, 2).astype(jnp.int32),
        "left_dims": ragged_sizes(part_keys[6], S, S * B * 3 // 4, B, 1).astype(jnp.int32),
        "right_dims": ragged_sizes(part_keys[7], S, S * W * 5 // 8, W, 1).astype(jnp.int32),
    }


group_size = 8

def apply_terms(vector, left_ops, right_ops, term_source, term_target, active, support):

    def add_group(accum, block_index):
        offset = block_index * group_size
        sources = lax.dynamic_slice_in_dim(term_source, offset, group_size, 0)
        targets = lax.dynamic_slice_in_dim(term_target, offset, group_size, 0)
        weights = lax.dynamic_slice_in_dim(active, offset, group_size, 0)
        left_group = lax.dynamic_slice_in_dim(left_ops, offset, group_size, 0).astype(jnp.float32)
        right_group = lax.dynamic_slice_in_dim(right_ops, offset, group_size, 0).astype(jnp.float32)
        blocks = vector[sources].astype(jnp.float32)
        inner_part = jnp.einsum('gkb,gbc->gkc', blocks, left_group, precision=lax.Precision.HIGHEST)
        term_out = jnp.einsum('gwk,gkc->gwc', right_group, inner_part, precision=lax.Precision.HIGHEST)
        return (accum.at[targets].add(term_out * weights[:, None, None]), None)
    start_sum = jnp.zeros((S, W, B), jnp.float32)
    summed, _ = lax.scan(add_group, start_sum, jnp.arange(TERMS // group_size, dtype=jnp.int32))
    return summed * support

def reference(wavefunction, left_ops, right_ops, term_source, term_target, term_count, left_dims, right_dims):
    support = ((jnp.arange(W, dtype=jnp.int32)[None, :, None] < right_dims[:, None, None]) & (jnp.arange(B, dtype=jnp.int32)[None, None, :] < left_dims[:, None, None])).astype(jnp.float32)
    slot_ids = jnp.arange(TERMS, dtype=jnp.int32)
    active = (slot_ids % P_DEV < term_count[slot_ids // P_DEV]).astype(jnp.float32)
    vectors = [(wavefunction.astype(jnp.float32) * support).astype(jnp.bfloat16)]
    results = []
    for step in range(STEPS):
        sigma = apply_terms(vectors[step], left_ops, right_ops, term_source, term_target, active, support)
        results.append(sigma)
        if step + 1 < STEPS:
            remainder = sigma
            wide = [entry.astype(jnp.float32) for entry in vectors]
            correlations = [jnp.sum(entry * sigma) for entry in wide]
            norms = [jnp.sum(entry * entry) for entry in wide]
            for entry, correlation, norm_value in zip(wide, correlations, norms):
                remainder = remainder - correlation / (norm_value + 1e-06) * entry
            mean_sq = jnp.sum(remainder * remainder) / (S * W * B)
            vectors.append((remainder * lax.rsqrt(mean_sq + 1e-06)).astype(jnp.bfloat16))
    return jnp.stack(results)
```

```python
import functools

import jax
import jax.numpy as jnp
from jax import lax
from jax.experimental import pallas as pl
from jax.experimental.pallas import tpu as pltpu
from jax.sharding import PartitionSpec as P

MESH = pl.DeviceIdType.MESH
steps = 3
group = 8
full_code = 32440.0


def kernel(
    row_total, col_total,
    source_ref, prev_ref, last_ref, left_dim_ref, right_dim_ref,
    wave_ref, left_hbm, right_hbm,
    out_ref,
    left_ref, right_ref, vec, own_vec, accum, send_code, recv_code, send_sums, recv_sums,
    load_sem, sums_send, sums_recv, code_send, code_recv,
    z_send, z_recv, x_send, x_recv, near_send, near_recv, far_send, far_recv,
):
    sectors, own_cols, left_size = wave_ref.shape
    slots = left_ref.shape[0]
    per_row = sectors // row_total
    block_rows = per_row * own_cols
    peers = row_total * col_total
    row = lax.axis_index("row")
    col = lax.axis_index("col")
    flat = row * col_total + col
    x_col = (col + col_total // 2) % col_total
    near_col = col + 1 - 2 * (col % 2)
    cell_total = sectors * own_cols * col_total * left_size

    def peer(n):
        place = (flat + n) % peers
        return {"row": place // col_total, "col": place % col_total}

    loads = [
        pltpu.make_async_copy(left_hbm, left_ref, load_sem.at[0]),
        pltpu.make_async_copy(right_hbm, right_ref, load_sem.at[1]),
    ]
    for load in loads:
        load.start()

    barrier = pltpu.get_barrier_semaphore()

    @pl.loop(1, peers)
    def _(n):
        pl.semaphore_signal(barrier, inc=1, device_id=peer(n), device_id_type=MESH)

    row_ids = lax.broadcasted_iota(jnp.int32, (own_cols, left_size), 0) + col * own_cols
    lane_ids = lax.broadcasted_iota(jnp.int32, (own_cols, left_size), 1)

    def support(s):
        return (row_ids < right_dim_ref[s]) & (lane_ids < left_dim_ref[s])

    @pl.loop(0, sectors)
    def _(s):
        value = wave_ref[s].astype(jnp.float32)
        vec[col, s] = jnp.where(support(s), value, 0.0).astype(jnp.bfloat16)

    @pl.loop(0, per_row)
    def _(j):
        own_vec[0, j] = vec[col, row * per_row + j]

    accum[slots] = jnp.zeros((own_cols, left_size), jnp.float32)
    pl.semaphore_wait(barrier, peers - 1)

    def block_of(which, d):
        place = (row + row_total - d) % row_total
        return vec.at[which, pl.ds(place * per_row, per_row)]

    def move(which, d, send, recv, row_to, col_to):
        ref = block_of(which, d)
        return pltpu.make_async_remote_copy(
            src_ref=ref, dst_ref=ref, send_sem=send.at[d], recv_sem=recv.at[d],
            device_id={"row": row_to, "col": col_to}, device_id_type=MESH,
        )

    def z_move(d):
        ref = block_of(col, 0)
        return pltpu.make_async_remote_copy(
            src_ref=ref, dst_ref=ref, send_sem=z_send.at[d], recv_sem=z_recv.at[d],
            device_id={"row": (row + d) % row_total, "col": col}, device_id_type=MESH,
        )

    def x_move(d):
        return move(col, d, x_send, x_recv, row, x_col)

    def near_move(d):
        return move(col, d, near_send, near_recv, row, near_col)

    def far_move(d):
        return move(x_col, d, far_send, far_recv, row, near_col)

    def spread(first):
        x_move(0).start()
        if not first:
            @pl.loop(1, row_total)
            def _(d):
                z_move(d).start()
        near_move(0).start()

        @pl.loop(1, row_total)
        def _(d):
            if not first:
                z_move(d).wait_recv()
            x_move(d).start()
            near_move(d).start()

        @pl.loop(0, row_total)
        def _(d):
            x_move(d).wait_recv()
            far_move(d).start()

        @pl.loop(0, row_total)
        def _(d):
            near_move(d).wait()
            far_move(d).wait()
            x_move(d).wait_send()

        if not first:
            @pl.loop(1, row_total)
            def _(d):
                z_move(d).wait_send()

    def apply_terms():
        @pl.loop(0, slots // group)
        def _(g):
            outs = []
            for i in range(group):
                p = g * group + i
                block = vec[:, source_ref[p]].reshape(col_total * own_cols, left_size)
                part = jnp.dot(right_ref[p], block, preferred_element_type=jnp.float32)
                high = part.astype(jnp.bfloat16)
                low = (part - high.astype(jnp.float32)).astype(jnp.bfloat16)
                both = jnp.dot(
                    jnp.concatenate([high, low], axis=0), left_ref[p],
                    preferred_element_type=jnp.float32,
                )
                outs.append(both[:own_cols] + both[own_cols:])
            for i in range(group):
                p = g * group + i
                accum[p] = outs[i] + accum[prev_ref[p]]

    def code_move(d):
        return pltpu.make_async_remote_copy(
            src_ref=send_code.at[d], dst_ref=recv_code.at[d],
            send_sem=code_send.at[d], recv_sem=code_recv.at[d],
            device_id={"row": (row + d) % row_total, "col": col}, device_id_type=MESH,
        )

    def sums_move(n):
        return pltpu.make_async_remote_copy(
            src_ref=send_sums, dst_ref=recv_sums.at[n],
            send_sem=sums_send.at[n], recv_sem=sums_recv.at[n],
            device_id=peer(n), device_id_type=MESH,
        )

    def send_partials():
        def peak(s, top):
            return jnp.maximum(top, jnp.abs(accum[last_ref[s]]))

        top = lax.fori_loop(
            0, sectors, peak, jnp.full((own_cols, left_size), 1e-30, jnp.float32)
        )
        level = jnp.ceil(jnp.log2(jnp.max(top, axis=(0, 1), keepdims=True)))
        factor = jnp.exp2(-level) * full_code
        tail = jnp.broadcast_to(level, (16, left_size)).astype(jnp.int32).astype(jnp.int16)

        @pl.loop(1, row_total)
        def _(d):
            base = ((row + d) % row_total) * per_row
            send_code[d, pl.ds(block_rows, 16)] = tail

            @pl.loop(0, per_row)
            def _(j):
                value = jnp.round(accum[last_ref[base + j]] * factor)
                send_code[d, pl.ds(pl.multiple_of(j * own_cols, 16), own_cols)] = value.astype(
                    jnp.int32
                ).astype(jnp.int16)

            code_move(d).start()

    def add_partials(step):
        def scale_of(d):
            level = recv_code[d, pl.ds(block_rows, 16)].astype(jnp.int32).astype(jnp.float32)
            return jnp.exp2(level[0:1, :]) * (1.0 / full_code)

        @pl.loop(0, per_row)
        def _(j):
            out_ref[step, j] = accum[last_ref[row * per_row + j]]

        @pl.loop(1, row_total)
        def _(d):
            code_move(d).wait_recv()
            scale = scale_of(d)

            @pl.loop(0, per_row)
            def _(j):
                code = recv_code[d, pl.ds(pl.multiple_of(j * own_cols, 16), own_cols)]
                out_ref[step, j] += code.astype(jnp.int32).astype(jnp.float32) * scale

        @pl.loop(0, per_row)
        def _(j):
            out_ref[step, j] = jnp.where(support(row * per_row + j), out_ref[step, j], 0.0)

    def fold(value):
        return jnp.sum(value, axis=0, keepdims=True)

    spread(True)
    for load in loads:
        load.wait()
    grams = {}
    for step in range(steps):
        apply_terms()
        send_partials()
        add_partials(step)

        @pl.loop(1, row_total)
        def _(d):
            code_move(d).wait_send()

        if step + 1 == steps:
            break
        pairs = [(i, step) for i in range(step + 1)]
        count = 1 + (step + 1) + len(pairs)

        def add_sums(j, totals):
            sigma = out_ref[step, j]
            wide = [own_vec[i, j].astype(jnp.float32) for i in range(step + 1)]
            items = [sigma * sigma] + [entry * sigma for entry in wide]
            items += [wide[i] * wide[k] for i, k in pairs]
            return tuple(a + b for a, b in zip(totals, items))

        zero = jnp.zeros((own_cols, left_size), jnp.float32)
        totals = lax.fori_loop(0, per_row, add_sums, (zero,) * count)
        rows = [fold(total) for total in totals]
        rows += [jnp.zeros((8 - count, left_size), jnp.float32)]
        send_sums[...] = jnp.concatenate(rows, axis=0)

        @pl.loop(1, peers)
        def _(n):
            sums_move(n).start()

        def gather_sums(n, total):
            sums_move(n).wait()
            return total + recv_sums[n]

        total = lax.fori_loop(1, peers, gather_sums, send_sums[...])
        total = jnp.sum(total, axis=1, keepdims=True)
        values = [total[i : i + 1] for i in range(count)]
        square, correlations = values[0], values[1 : step + 2]
        for pair, value in zip(pairs, values[step + 2 :]):
            grams[pair] = value
        weights = [
            correlations[i] / (grams[(i, i)] + 1e-06) for i in range(step + 1)
        ]
        for i in range(step + 1):
            square = square - 2.0 * weights[i] * correlations[i]
            for k in range(step + 1):
                square = square + weights[i] * weights[k] * grams[(min(i, k), max(i, k))]
        mean_sq = jnp.maximum(square, 0.0) / cell_total
        factor = lax.rsqrt(mean_sq + 1e-06)

        @pl.loop(0, per_row)
        def _(j):
            remainder = out_ref[step, j]
            for i in range(step + 1):
                remainder = remainder - weights[i] * own_vec[i, j].astype(jnp.float32)
            fresh = (remainder * factor).astype(jnp.bfloat16)
            vec[col, row * per_row + j] = fresh
            if step + 2 < steps:
                own_vec[step + 1, j] = fresh

        spread(False)


def body(
    wavefunction, left_ops, right_ops, term_source, term_target, term_count, left_dims, right_dims
):
    row_total = lax.axis_size("row")
    col_total = lax.axis_size("col")
    peers = row_total * col_total
    sectors, own_cols, left_size = wavefunction.shape
    slots = left_ops.shape[0]
    per_row = sectors // row_total
    ids = jnp.arange(slots, dtype=jnp.int32)
    active = ids < term_count[0]
    same = (
        (term_target[:, None] == term_target[None, :])
        & active[None, :]
        & (ids[None, :] < ids[:, None])
    )
    prev = jnp.max(jnp.where(same, ids[None, :], -1), axis=1)
    prev = jnp.where(prev < 0, slots, prev)
    here = (jnp.arange(sectors, dtype=jnp.int32)[:, None] == term_target[None, :]) & active[None, :]
    last = jnp.max(jnp.where(here, ids[None, :], -1), axis=1)
    last = jnp.where(last < 0, slots, last)
    code_rows = per_row * own_cols + 16
    smem = pl.BlockSpec(memory_space=pltpu.SMEM)
    vmem = pl.BlockSpec(memory_space=pltpu.VMEM)
    hbm = pl.BlockSpec(memory_space=pl.ANY)
    dma = pltpu.SemaphoreType.DMA
    return pl.pallas_call(
        functools.partial(kernel, row_total, col_total),
        out_shape=jax.ShapeDtypeStruct((steps, per_row, own_cols, left_size), jnp.float32),
        in_specs=[smem] * 5 + [vmem, hbm, hbm],
        out_specs=vmem,
        scratch_shapes=[
            pltpu.VMEM(left_ops.shape, jnp.bfloat16),
            pltpu.VMEM(right_ops.shape, jnp.bfloat16),
            pltpu.VMEM((col_total, sectors, own_cols, left_size), jnp.bfloat16),
            pltpu.VMEM((2, per_row, own_cols, left_size), jnp.bfloat16),
            pltpu.VMEM((slots + 1, own_cols, left_size), jnp.float32),
            pltpu.VMEM((row_total, code_rows, left_size), jnp.int16),
            pltpu.VMEM((row_total, code_rows, left_size), jnp.int16),
            pltpu.VMEM((8, left_size), jnp.float32),
            pltpu.VMEM((peers, 8, left_size), jnp.float32),
            dma((2,)),
            dma((peers,)),
            dma((peers,)),
        ]
        + [dma((row_total,))] * 10,
        compiler_params=pltpu.CompilerParams(
            collective_id=0, has_side_effects=True, vmem_limit_bytes=40 * 1024 * 1024
        ),
        cost_estimate=pl.CostEstimate(
            flops=steps * slots * 6 * own_cols * left_size * left_size,
            bytes_accessed=8 * 1024 * 1024,
            transcendentals=0,
        ),
    )(term_source, prev, last, left_dims, right_dims, wavefunction, left_ops, right_ops)


def solution(mesh):
    placed = (
        P("parts", "col", None),
        P(("parts", "row"), None, None),
        P(("parts", "row"), "col", None),
        P(("parts", "row")),
        P(("parts", "row")),
        P(("parts", "row")),
        P("parts"),
        P("parts"),
    )
    return jax.shard_map(
        body,
        mesh=mesh,
        in_specs=placed,
        out_specs=P(None, ("parts", "row"), "col", None),
        check_vma=False,
    )
```

```python
import functools

import jax
import jax.numpy as jnp
from jax import lax
from jax.experimental import pallas as pl
from jax.experimental.pallas import tpu as pltpu
from jax.sharding import PartitionSpec as P

MESH = pl.DeviceIdType.MESH
steps = 3
group = 8
full_code = 32440.0
pieces, shared = 8, 3


def kernel(
    row_total, col_total,
    source_ref, prev_ref, last_ref, left_dim_ref, right_dim_ref,
    wave_ref, left_hbm, right_hbm,
    out_ref,
    left_ref, right_ref, vec, own_vec, accum, total_block, send_code, recv_code, send_sums, recv_sums,
    load_sem, sums_send, sums_recv, code_send, code_recv,
    z_send, z_recv, x_send, x_recv, near_send, near_recv, far_send, far_recv,
):
    sectors, own_cols, left_size = wave_ref.shape
    slots = left_ref.shape[0]
    per_row = sectors // row_total
    block_rows = per_row * own_cols
    halves = 2 if per_row % 2 == 0 else 1
    unroll = 4 if per_row % 4 == 0 else 1
    peers = row_total * col_total
    row = lax.axis_index("row")
    col = lax.axis_index("col")
    flat = row * col_total + col
    x_col = (col + col_total // 2) % col_total
    near_col = col + 1 - 2 * (col % 2)
    cell_total = sectors * own_cols * col_total * left_size

    def peer(n):
        place = (flat + n) % peers
        return {"row": place // col_total, "col": place % col_total}

    loads = [
        pltpu.make_async_copy(left_hbm, left_ref, load_sem.at[0]),
        pltpu.make_async_copy(right_hbm, right_ref, load_sem.at[1]),
    ]
    for load in loads:
        load.start()

    barrier = pltpu.get_barrier_semaphore()

    @pl.loop(1, peers)
    def _(n):
        pl.semaphore_signal(barrier, inc=1, device_id=peer(n), device_id_type=MESH)

    row_ids = lax.broadcasted_iota(jnp.int32, (own_cols, left_size), 0) + col * own_cols
    lane_ids = lax.broadcasted_iota(jnp.int32, (own_cols, left_size), 1)

    def support(s):
        return (row_ids < right_dim_ref[s]) & (lane_ids < left_dim_ref[s])

    @pl.loop(0, sectors)
    def _(s):
        value = wave_ref[s].astype(jnp.float32)
        vec[col, s] = jnp.where(support(s), value, 0.0).astype(jnp.bfloat16)

    @pl.loop(0, per_row)
    def _(j):
        own_vec[0, j] = vec[col, row * per_row + j]

    accum[slots] = jnp.zeros((own_cols, left_size), jnp.float32)
    pl.semaphore_wait(barrier, peers - 1)

    def move(which, start, size, send, recv, row_to, col_to):
        ref = vec.at[which, pl.ds(start, size)]
        return pltpu.make_async_remote_copy(
            src_ref=ref, dst_ref=ref, send_sem=send, recv_sem=recv,
            device_id={"row": row_to, "col": col_to}, device_id_type=MESH,
        )

    def mirror(r):
        return jnp.where(row < 2, r, 3 - r)

    def spread_first():
        size = sectors // pieces
        side = row % 2
        alone = [side * shared + i for i in range(shared)]
        other = [(1 - side) * shared + i for i in range(shared)]
        common = list(range(2 * shared, pieces))

        def x_move(k):
            return move(col, k * size, size, x_send.at[k], x_recv.at[k], row, x_col)

        def pair_move(k):
            return move(
                x_col, k * size, size, z_send.at[k], z_recv.at[k], row + 1 - 2 * side, col
            )

        def near_move():
            return move(col, 0, sectors, near_send.at[0], near_recv.at[0], row, near_col)

        def far_move(k):
            return move(x_col, k * size, size, far_send.at[k], far_recv.at[k], row, near_col)

        for k in alone + common:
            x_move(k).start()
        near_move().start()
        for k in alone:
            x_move(k).wait_recv()
            pair_move(k).start()
            far_move(k).start()
        for mine, theirs in zip(common + [None] * shared, other):
            if mine is not None:
                x_move(mine).wait_recv()
                far_move(mine).start()
            pair_move(theirs).wait_recv()
            far_move(theirs).start()
        for k in alone + common:
            x_move(k).wait_send()
        for k in alone:
            pair_move(k).wait_send()
        near_move().wait()

        @pl.loop(0, pieces)
        def _(k):
            far_move(k).wait()

    def spread():
        size = per_row // halves

        def part(which, b, h, send, recv, k, row_to, col_to):
            return move(
                which, b * per_row + h * size, size, send.at[k * halves + h],
                recv.at[b * halves + h], row_to, col_to,
            )

        def z_move(to, h):
            return part(col, row, h, z_send, z_recv, to, to, col)

        def z_arrival(b, h):
            return part(col, b, h, z_send, z_recv, b, row, near_col)

        def relay_move(h):
            return part(col, mirror(2), h, z_send, z_recv, row_total, mirror(0), col)

        def x_move(b, h):
            return part(col, b, h, x_send, x_recv, b, row, x_col)

        def near_move(b, h):
            return part(col, b, h, near_send, near_recv, b, row, near_col)

        def far_move(b, h):
            return part(x_col, b, h, far_send, far_recv, b, row, near_col)

        def start_all(b, h):
            x_move(b, h).start()
            near_move(b, h).start()

        def arrived(b, relay=False):
            for h in range(halves):
                z_arrival(b, h).wait_recv()
                if relay:
                    @pl.when(middle)
                    def _():
                        relay_move(h).start()
                start_all(b, h)

        def x_arrived(b):
            for h in range(halves):
                x_move(b, h).wait_recv()
                far_move(b, h).start()

        for h in range(halves):
            x_move(row, h).start()
        if row_total == 4:
            middle = (row == 1) | (row == 2)
            inner = middle.astype(jnp.int32)
            order = [mirror(1 + inner), mirror(3 - 3 * inner), mirror(2 + inner)]
            sends = [mirror(3 - inner), mirror(2 - 2 * inner)]
            for to in sends:
                for h in range(halves):
                    z_move(to, h).start()

            @pl.when(jnp.logical_not(middle))
            def _():
                for h in range(halves):
                    z_move(mirror(1), h).start()

            for h in range(halves):
                near_move(row, h).start()
            arrived(order[0], True)
            x_arrived(row)
            arrived(order[1])
            x_arrived(order[0])
            arrived(order[2])
            x_arrived(order[1])
            x_arrived(order[2])
            for h in range(halves):
                for to in sends:
                    z_move(to, h).wait_send()

                @pl.when(jnp.logical_not(middle))
                def _():
                    z_move(mirror(1), h).wait_send()

                @pl.when(middle)
                def _():
                    relay_move(h).wait_send()
        else:
            @pl.loop(1, row_total)
            def _(d):
                for h in range(halves):
                    z_move((row + d) % row_total, h).start()

            for h in range(halves):
                near_move(row, h).start()

            @pl.loop(1, row_total)
            def _(d):
                arrived((row + row_total - d) % row_total)

            @pl.loop(0, row_total)
            def _(b):
                x_arrived(b)

            @pl.loop(1, row_total)
            def _(d):
                for h in range(halves):
                    z_move((row + d) % row_total, h).wait_send()

        @pl.loop(0, row_total)
        def _(b):
            for h in range(halves):
                near_move(b, h).wait()
                far_move(b, h).wait()
                x_move(b, h).wait_send()

    def apply_terms():
        @pl.loop(0, slots // group)
        def _(g):
            outs = []
            for i in range(group):
                p = g * group + i
                block = vec[:, source_ref[p]].reshape(col_total * own_cols, left_size)
                part = jnp.dot(right_ref[p], block, preferred_element_type=jnp.float32)
                high = part.astype(jnp.bfloat16)
                low = (part - high.astype(jnp.float32)).astype(jnp.bfloat16)
                both = jnp.dot(
                    jnp.concatenate([high, low], axis=0), left_ref[p],
                    preferred_element_type=jnp.float32,
                )
                outs.append(both[:own_cols] + both[own_cols:])
            for i in range(group):
                p = g * group + i
                accum[p] = outs[i] + accum[prev_ref[p]]

    def code_move(o, slot, row_to):
        return pltpu.make_async_remote_copy(
            src_ref=send_code.at[o], dst_ref=recv_code.at[slot],
            send_sem=code_send.at[o], recv_sem=code_recv.at[slot],
            device_id={"row": row_to, "col": col}, device_id_type=MESH,
        )

    def sums_move(n):
        return pltpu.make_async_remote_copy(
            src_ref=send_sums, dst_ref=recv_sums.at[n],
            send_sem=sums_send.at[n], recv_sem=sums_recv.at[n],
            device_id=peer(n), device_id_type=MESH,
        )

    def scale_of(slot):
        level = recv_code[slot, pl.ds(block_rows, 16)].astype(jnp.int32).astype(jnp.float32)
        return jnp.exp2(level[0:1, :]) * (1.0 / full_code)

    def rows_of(j):
        return pl.ds(pl.multiple_of(j * own_cols, 16), own_cols)

    def decode(slot, j, scale):
        return recv_code[slot, rows_of(j)].astype(jnp.int32).astype(jnp.float32) * scale

    def relay(o, slot, first):
        scale = None if first else scale_of(slot)

        def gather(j, top):
            value = accum[last_ref[o * per_row + j]]
            if not first:
                value = value + decode(slot, j, scale)
            total_block[j] = value
            return jnp.maximum(top, jnp.abs(value))

        top = lax.fori_loop(
            0, per_row, gather, jnp.full((own_cols, left_size), 1e-30, jnp.float32),
            unroll=unroll,
        )
        level = jnp.ceil(jnp.log2(jnp.max(top, axis=(0, 1), keepdims=True)))
        factor = jnp.exp2(-level) * full_code
        send_code[o, pl.ds(block_rows, 16)] = (
            jnp.broadcast_to(level, (16, left_size)).astype(jnp.int32).astype(jnp.int16)
        )

        @pl.loop(0, per_row, unroll=unroll)
        def _(j):
            value = jnp.round(total_block[j] * factor)
            send_code[o, rows_of(j)] = value.astype(jnp.int32).astype(jnp.int16)

    def reduce_partials(step):
        def send(o):
            relay(o, 0, True)
            code_move(o, row, o).start()

        def receive(r):
            code_move(row, r, near_row).wait_recv()
            scale = scale_of(r)

            @pl.loop(0, per_row, unroll=unroll)
            def _(j):
                out_ref[step, j] += decode(r, j, scale)

        near_row = (row + 1) % row_total

        def take_own():
            @pl.loop(0, per_row, unroll=unroll)
            def _(j):
                out_ref[step, j] = accum[last_ref[row * per_row + j]]

        if row_total == 4:
            middle = (row == 1) | (row == 2)
            end = jnp.logical_not(middle)

            @pl.when(end)
            def _():
                relay(mirror(3), 0, True)
                code_move(mirror(3), row_total, mirror(1)).start()
                send(mirror(2))
                send(mirror(1))

            @pl.when(middle)
            def _():
                send(mirror(2))
                send(mirror(0))
                code_move(row, row_total, near_row).wait_recv()
                relay(mirror(3), row_total, False)
                code_move(mirror(3), row, mirror(3)).start()

            take_own()

            @pl.when(end)
            def _():
                receive(mirror(1))
                receive(mirror(2))

            @pl.when(middle)
            def _():
                receive(mirror(2))
                receive(mirror(0))
                receive(mirror(3))
        else:
            @pl.loop(1, row_total)
            def _(d):
                send((row + d) % row_total)

            take_own()

            @pl.loop(1, row_total)
            def _(d):
                receive((row + row_total - d) % row_total)

        @pl.loop(0, per_row, unroll=unroll)
        def _(j):
            out_ref[step, j] = jnp.where(support(row * per_row + j), out_ref[step, j], 0.0)

        @pl.loop(1, row_total)
        def _(d):
            o = (row + d) % row_total
            code_move(o, row, near_row).wait_send()

    def fold(value):
        return jnp.sum(value, axis=0, keepdims=True)

    spread_first()
    for load in loads:
        load.wait()
    grams = {}
    for step in range(steps):
        apply_terms()
        reduce_partials(step)

        if step + 1 == steps:
            break
        pairs = [(i, step) for i in range(step + 1)]
        count = 1 + (step + 1) + len(pairs)

        def add_sums(j, totals):
            sigma = out_ref[step, j]
            wide = [own_vec[i, j].astype(jnp.float32) for i in range(step + 1)]
            items = [sigma * sigma] + [entry * sigma for entry in wide]
            items += [wide[i] * wide[k] for i, k in pairs]
            return tuple(a + b for a, b in zip(totals, items))

        zero = jnp.zeros((own_cols, left_size), jnp.float32)
        totals = lax.fori_loop(0, per_row, add_sums, (zero,) * count, unroll=unroll)
        rows = [fold(total) for total in totals]
        rows += [jnp.zeros((8 - count, left_size), jnp.float32)]
        send_sums[...] = jnp.concatenate(rows, axis=0)

        @pl.loop(1, peers)
        def _(n):
            sums_move(n).start()

        def gather_sums(n, total):
            sums_move(n).wait()
            return total + recv_sums[n]

        total = lax.fori_loop(1, peers, gather_sums, send_sums[...])
        total = jnp.sum(total, axis=1, keepdims=True)
        values = [total[i : i + 1] for i in range(count)]
        square, correlations = values[0], values[1 : step + 2]
        for pair, value in zip(pairs, values[step + 2 :]):
            grams[pair] = value
        weights = [
            correlations[i] / (grams[(i, i)] + 1e-06) for i in range(step + 1)
        ]
        for i in range(step + 1):
            square = square - 2.0 * weights[i] * correlations[i]
            for k in range(step + 1):
                square = square + weights[i] * weights[k] * grams[(min(i, k), max(i, k))]
        mean_sq = jnp.maximum(square, 0.0) / cell_total
        factor = lax.rsqrt(mean_sq + 1e-06)

        @pl.loop(0, per_row)
        def _(j):
            remainder = out_ref[step, j]
            for i in range(step + 1):
                remainder = remainder - weights[i] * own_vec[i, j].astype(jnp.float32)
            fresh = (remainder * factor).astype(jnp.bfloat16)
            vec[col, row * per_row + j] = fresh
            if step + 2 < steps:
                own_vec[step + 1, j] = fresh

        spread()


def body(
    wavefunction, left_ops, right_ops, term_source, term_target, term_count, left_dims, right_dims
):
    row_total = lax.axis_size("row")
    col_total = lax.axis_size("col")
    peers = row_total * col_total
    sectors, own_cols, left_size = wavefunction.shape
    slots = left_ops.shape[0]
    per_row = sectors // row_total
    ids = jnp.arange(slots, dtype=jnp.int32)
    active = ids < term_count[0]
    same = (
        (term_target[:, None] == term_target[None, :])
        & active[None, :]
        & (ids[None, :] < ids[:, None])
    )
    prev = jnp.max(jnp.where(same, ids[None, :], -1), axis=1)
    prev = jnp.where(prev < 0, slots, prev)
    here = (jnp.arange(sectors, dtype=jnp.int32)[:, None] == term_target[None, :]) & active[None, :]
    last = jnp.max(jnp.where(here, ids[None, :], -1), axis=1)
    last = jnp.where(last < 0, slots, last)
    code_rows = per_row * own_cols + 16
    smem = pl.BlockSpec(memory_space=pltpu.SMEM)
    vmem = pl.BlockSpec(memory_space=pltpu.VMEM)
    hbm = pl.BlockSpec(memory_space=pl.ANY)
    dma = pltpu.SemaphoreType.DMA
    return pl.pallas_call(
        functools.partial(kernel, row_total, col_total),
        out_shape=jax.ShapeDtypeStruct((steps, per_row, own_cols, left_size), jnp.float32),
        in_specs=[smem] * 5 + [vmem, hbm, hbm],
        out_specs=vmem,
        scratch_shapes=[
            pltpu.VMEM(left_ops.shape, jnp.bfloat16),
            pltpu.VMEM(right_ops.shape, jnp.bfloat16),
            pltpu.VMEM((col_total, sectors, own_cols, left_size), jnp.bfloat16),
            pltpu.VMEM((2, per_row, own_cols, left_size), jnp.bfloat16),
            pltpu.VMEM((slots + 1, own_cols, left_size), jnp.float32),
            pltpu.VMEM((per_row, own_cols, left_size), jnp.float32),
            pltpu.VMEM((row_total, code_rows, left_size), jnp.int16),
            pltpu.VMEM((row_total + 1, code_rows, left_size), jnp.int16),
            pltpu.VMEM((8, left_size), jnp.float32),
            pltpu.VMEM((peers, 8, left_size), jnp.float32),
            dma((2,)),
            dma((peers,)),
            dma((peers,)),
        ]
        + [dma((row_total + 1,))] * 2
        + [dma((max(pieces, 2 * row_total + 2),))] * 8,
        compiler_params=pltpu.CompilerParams(
            collective_id=0, has_side_effects=True, vmem_limit_bytes=58 * 1024 * 1024
        ),
        cost_estimate=pl.CostEstimate(
            flops=steps * slots * 6 * own_cols * left_size * left_size,
            bytes_accessed=8 * 1024 * 1024,
            transcendentals=0,
        ),
    )(term_source, prev, last, left_dims, right_dims, wavefunction, left_ops, right_ops)


def solution(mesh):
    placed = (
        P("parts", "col", None),
        P(("parts", "row"), None, None),
        P(("parts", "row"), "col", None),
        P(("parts", "row")),
        P(("parts", "row")),
        P(("parts", "row")),
        P("parts"),
        P("parts"),
    )
    return jax.shard_map(
        body,
        mesh=mesh,
        in_specs=placed,
        out_specs=P(None, ("parts", "row"), "col", None),
        check_vma=False,
    )
```

```python
import functools

import jax
import jax.numpy as jnp
from jax import lax
from jax.experimental import pallas as pl
from jax.experimental.pallas import tpu as pltpu
from jax.sharding import PartitionSpec as P

MESH = pl.DeviceIdType.MESH
steps = 3
group = 32
full_code = 32440.0
pieces, shared = 8, 3


def kernel(
    row_total, col_total,
    source_ref, prev_ref, last_ref, left_dim_ref, right_dim_ref,
    wave_ref, left_hbm, right_hbm,
    out_ref,
    left_ref, right_ref, vec, own_vec, accum, total_block, send_code, recv_code, send_sums, recv_sums,
    load_sem, sums_send, sums_recv, code_send, code_recv,
    z_send, z_recv, x_send, x_recv, near_send, near_recv, far_send, far_recv,
):
    sectors, own_cols, left_size = wave_ref.shape
    slots = left_ref.shape[0]
    per_row = sectors // row_total
    block_rows = per_row * own_cols
    halves = 2 if per_row % 2 == 0 else 1
    unroll = 4 if per_row % 4 == 0 else 1
    peers = row_total * col_total
    peer_unroll = 15 if (peers - 1) % 15 == 0 and peers <= 32 else 1
    row = lax.axis_index("row")
    col = lax.axis_index("col")
    flat = row * col_total + col
    x_col = (col + col_total // 2) % col_total
    near_col = col + 1 - 2 * (col % 2)
    cell_total = sectors * own_cols * col_total * left_size

    def peer(n):
        place = (flat + n) % peers
        return {"row": place // col_total, "col": place % col_total}

    loads = [
        pltpu.make_async_copy(left_hbm, left_ref, load_sem.at[0]),
        pltpu.make_async_copy(right_hbm, right_ref, load_sem.at[1]),
    ]
    for load in loads:
        load.start()

    barrier = pltpu.get_barrier_semaphore()

    @pl.loop(1, peers)
    def _(n):
        pl.semaphore_signal(barrier, inc=1, device_id=peer(n), device_id_type=MESH)

    row_ids = lax.broadcasted_iota(jnp.int32, (own_cols, left_size), 0) + col * own_cols
    lane_ids = lax.broadcasted_iota(jnp.int32, (own_cols, left_size), 1)

    def support(s):
        return (row_ids < right_dim_ref[s]) & (lane_ids < left_dim_ref[s])

    @pl.loop(0, sectors, unroll=4)
    def _(s):
        value = wave_ref[s].astype(jnp.float32)
        vec[col, s] = jnp.where(support(s), value, 0.0).astype(jnp.bfloat16)

    @pl.loop(0, per_row)
    def _(j):
        own_vec[0, j] = vec[col, row * per_row + j]

    accum[slots] = jnp.zeros((own_cols, left_size), jnp.float32)
    pl.semaphore_wait(barrier, peers - 1)

    def move(which, start, size, send, recv, row_to, col_to):
        ref = vec.at[which, pl.ds(start, size)]
        return pltpu.make_async_remote_copy(
            src_ref=ref, dst_ref=ref, send_sem=send, recv_sem=recv,
            device_id={"row": row_to, "col": col_to}, device_id_type=MESH,
        )

    def mirror(r):
        return jnp.where(row < 2, r, 3 - r)

    def spread_first():
        size = sectors // pieces
        side = row % 2
        alone = [side * shared + i for i in range(shared)]
        other = [(1 - side) * shared + i for i in range(shared)]
        common = list(range(2 * shared, pieces))

        def x_move(k):
            return move(col, k * size, size, x_send.at[k], x_recv.at[k], row, x_col)

        def pair_move(k):
            return move(
                x_col, k * size, size, z_send.at[k], z_recv.at[k], row + 1 - 2 * side, col
            )

        def near_move():
            return move(col, 0, sectors, near_send.at[0], near_recv.at[0], row, near_col)

        def far_move(k):
            return move(x_col, k * size, size, far_send.at[k], far_recv.at[k], row, near_col)

        for k in alone + common:
            x_move(k).start()
        near_move().start()
        for k in alone:
            x_move(k).wait_recv()
            pair_move(k).start()
            far_move(k).start()
        for mine, theirs in zip(common + [None] * shared, other):
            if mine is not None:
                x_move(mine).wait_recv()
                far_move(mine).start()
            pair_move(theirs).wait_recv()
            far_move(theirs).start()
        for k in alone + common:
            x_move(k).wait_send()
        for k in alone:
            pair_move(k).wait_send()
        near_move().wait()

        @pl.loop(0, pieces)
        def _(k):
            far_move(k).wait()

    def spread():
        size = per_row // halves

        def part(which, b, h, send, recv, k, row_to, col_to):
            return move(
                which, b * per_row + h * size, size, send.at[k * halves + h],
                recv.at[b * halves + h], row_to, col_to,
            )

        def z_move(to, h):
            return part(col, row, h, z_send, z_recv, to, to, col)

        def z_arrival(b, h):
            return part(col, b, h, z_send, z_recv, b, row, near_col)

        def relay_move(h):
            return part(col, mirror(2), h, z_send, z_recv, row_total, mirror(0), col)

        def x_move(b, h):
            return part(col, b, h, x_send, x_recv, b, row, x_col)

        def near_move(b, h):
            return part(col, b, h, near_send, near_recv, b, row, near_col)

        def far_move(b, h):
            return part(x_col, b, h, far_send, far_recv, b, row, near_col)

        def start_all(b, h):
            x_move(b, h).start()
            near_move(b, h).start()

        def arrived(b, relay=False):
            for h in range(halves):
                z_arrival(b, h).wait_recv()
                if relay:
                    @pl.when(middle)
                    def _():
                        relay_move(h).start()
                start_all(b, h)

        def x_arrived(b):
            for h in range(halves):
                x_move(b, h).wait_recv()
                far_move(b, h).start()

        for h in range(halves):
            x_move(row, h).start()
        if row_total == 4:
            middle = (row == 1) | (row == 2)
            inner = middle.astype(jnp.int32)
            order = [mirror(1 + inner), mirror(3 - 3 * inner), mirror(2 + inner)]
            sends = [mirror(3 - inner), mirror(2 - 2 * inner)]
            for to in sends:
                for h in range(halves):
                    z_move(to, h).start()

            @pl.when(jnp.logical_not(middle))
            def _():
                for h in range(halves):
                    z_move(mirror(1), h).start()

            for h in range(halves):
                near_move(row, h).start()
            arrived(order[0], True)
            x_arrived(row)
            arrived(order[1])
            x_arrived(order[0])
            arrived(order[2])
            x_arrived(order[1])
            x_arrived(order[2])
            for h in range(halves):
                for to in sends:
                    z_move(to, h).wait_send()

                @pl.when(jnp.logical_not(middle))
                def _():
                    z_move(mirror(1), h).wait_send()

                @pl.when(middle)
                def _():
                    relay_move(h).wait_send()
        else:
            @pl.loop(1, row_total)
            def _(d):
                for h in range(halves):
                    z_move((row + d) % row_total, h).start()

            for h in range(halves):
                near_move(row, h).start()

            @pl.loop(1, row_total)
            def _(d):
                arrived((row + row_total - d) % row_total)

            @pl.loop(0, row_total)
            def _(b):
                x_arrived(b)

            @pl.loop(1, row_total)
            def _(d):
                for h in range(halves):
                    z_move((row + d) % row_total, h).wait_send()

        @pl.loop(0, row_total)
        def _(b):
            for h in range(halves):
                near_move(b, h).wait()
                far_move(b, h).wait()
                x_move(b, h).wait_send()

    def apply_terms():
        @pl.loop(0, slots // group)
        def _(g):
            outs = []
            for i in range(group):
                p = g * group + i
                block = vec[:, source_ref[p]].reshape(col_total * own_cols, left_size)
                part = jnp.dot(right_ref[p], block, preferred_element_type=jnp.float32)
                high = part.astype(jnp.bfloat16)
                low = (part - high.astype(jnp.float32)).astype(jnp.bfloat16)
                both = jnp.dot(
                    jnp.concatenate([high, low], axis=0), left_ref[p],
                    preferred_element_type=jnp.float32,
                )
                outs.append(both[:own_cols] + both[own_cols:])
            for i in range(group):
                p = g * group + i
                accum[p] = outs[i] + accum[prev_ref[p]]

    def code_move(o, slot, row_to):
        return pltpu.make_async_remote_copy(
            src_ref=send_code.at[o], dst_ref=recv_code.at[slot],
            send_sem=code_send.at[o], recv_sem=code_recv.at[slot],
            device_id={"row": row_to, "col": col}, device_id_type=MESH,
        )

    def sums_move(n):
        return pltpu.make_async_remote_copy(
            src_ref=send_sums, dst_ref=recv_sums.at[n],
            send_sem=sums_send.at[n], recv_sem=sums_recv.at[n],
            device_id=peer(n), device_id_type=MESH,
        )

    def scale_of(slot):
        level = recv_code[slot, pl.ds(block_rows, 16)].astype(jnp.int32).astype(jnp.float32)
        return jnp.exp2(level[0:1, :]) * (1.0 / full_code)

    def rows_of(j):
        return pl.ds(pl.multiple_of(j * own_cols, 16), own_cols)

    def decode(slot, j, scale):
        return recv_code[slot, rows_of(j)].astype(jnp.int32).astype(jnp.float32) * scale

    def relay(o, slot, first):
        scale = None if first else scale_of(slot)

        def gather(j, top):
            value = accum[last_ref[o * per_row + j]]
            if not first:
                value = value + decode(slot, j, scale)
            total_block[j] = value
            return jnp.maximum(top, jnp.abs(value))

        top = lax.fori_loop(
            0, per_row, gather, jnp.full((own_cols, left_size), 1e-30, jnp.float32),
            unroll=unroll,
        )
        level = jnp.ceil(jnp.log2(jnp.max(top, axis=(0, 1), keepdims=True)))
        factor = jnp.exp2(-level) * full_code
        send_code[o, pl.ds(block_rows, 16)] = (
            jnp.broadcast_to(level, (16, left_size)).astype(jnp.int32).astype(jnp.int16)
        )

        @pl.loop(0, per_row, unroll=unroll)
        def _(j):
            value = jnp.round(total_block[j] * factor)
            send_code[o, rows_of(j)] = value.astype(jnp.int32).astype(jnp.int16)

    def reduce_partials(step):
        def send(o):
            relay(o, 0, True)
            code_move(o, row, o).start()

        def receive(r):
            code_move(row, r, near_row).wait_recv()
            scale = scale_of(r)

            @pl.loop(0, per_row, unroll=unroll)
            def _(j):
                out_ref[step, j] += decode(r, j, scale)

        near_row = (row + 1) % row_total

        def take_own():
            @pl.loop(0, per_row, unroll=unroll)
            def _(j):
                out_ref[step, j] = accum[last_ref[row * per_row + j]]

        if row_total == 4:
            middle = (row == 1) | (row == 2)
            end = jnp.logical_not(middle)

            @pl.when(end)
            def _():
                relay(mirror(3), 0, True)
                code_move(mirror(3), row_total, mirror(1)).start()
                send(mirror(2))
                send(mirror(1))

            @pl.when(middle)
            def _():
                send(mirror(2))
                send(mirror(0))
                code_move(row, row_total, near_row).wait_recv()
                relay(mirror(3), row_total, False)
                code_move(mirror(3), row, mirror(3)).start()

            take_own()

            @pl.when(end)
            def _():
                receive(mirror(1))
                receive(mirror(2))

            @pl.when(middle)
            def _():
                receive(mirror(2))
                receive(mirror(0))
                receive(mirror(3))
        else:
            @pl.loop(1, row_total)
            def _(d):
                send((row + d) % row_total)

            take_own()

            @pl.loop(1, row_total)
            def _(d):
                receive((row + row_total - d) % row_total)

        @pl.loop(0, per_row, unroll=unroll)
        def _(j):
            out_ref[step, j] = jnp.where(support(row * per_row + j), out_ref[step, j], 0.0)

        @pl.loop(1, row_total)
        def _(d):
            o = (row + d) % row_total
            code_move(o, row, near_row).wait_send()

    def fold(value):
        return jnp.sum(value, axis=0, keepdims=True)

    spread_first()
    for load in loads:
        load.wait()
    grams = {}
    for step in range(steps):
        apply_terms()
        reduce_partials(step)

        if step + 1 == steps:
            break
        pairs = [(i, step) for i in range(step + 1)]
        count = 1 + (step + 1) + len(pairs)

        def add_sums(j, totals):
            sigma = out_ref[step, j]
            wide = [own_vec[i, j].astype(jnp.float32) for i in range(step + 1)]
            items = [sigma * sigma] + [entry * sigma for entry in wide]
            items += [wide[i] * wide[k] for i, k in pairs]
            return tuple(a + b for a, b in zip(totals, items))

        zero = jnp.zeros((own_cols, left_size), jnp.float32)
        totals = lax.fori_loop(0, per_row, add_sums, (zero,) * count, unroll=unroll)
        rows = [fold(total) for total in totals]
        rows += [jnp.zeros((8 - count, left_size), jnp.float32)]
        send_sums[...] = jnp.concatenate(rows, axis=0)

        @pl.loop(1, peers, unroll=peer_unroll)
        def _(n):
            sums_move(n).start()

        def gather_sums(n, total):
            sums_move(n).wait()
            return total + recv_sums[n]

        total = lax.fori_loop(1, peers, gather_sums, send_sums[...], unroll=peer_unroll)
        total = jnp.sum(total, axis=1, keepdims=True)
        values = [total[i : i + 1] for i in range(count)]
        square, correlations = values[0], values[1 : step + 2]
        for pair, value in zip(pairs, values[step + 2 :]):
            grams[pair] = value
        weights = [
            correlations[i] / (grams[(i, i)] + 1e-06) for i in range(step + 1)
        ]
        for i in range(step + 1):
            square = square - 2.0 * weights[i] * correlations[i]
            for k in range(step + 1):
                square = square + weights[i] * weights[k] * grams[(min(i, k), max(i, k))]
        mean_sq = jnp.maximum(square, 0.0) / cell_total
        factor = lax.rsqrt(mean_sq + 1e-06)

        @pl.loop(0, per_row)
        def _(j):
            remainder = out_ref[step, j]
            for i in range(step + 1):
                remainder = remainder - weights[i] * own_vec[i, j].astype(jnp.float32)
            fresh = (remainder * factor).astype(jnp.bfloat16)
            vec[col, row * per_row + j] = fresh
            if step + 2 < steps:
                own_vec[step + 1, j] = fresh

        spread()


def body(
    wavefunction, left_ops, right_ops, term_source, term_target, term_count, left_dims, right_dims
):
    row_total = lax.axis_size("row")
    col_total = lax.axis_size("col")
    peers = row_total * col_total
    sectors, own_cols, left_size = wavefunction.shape
    slots = left_ops.shape[0]
    per_row = sectors // row_total
    ids = jnp.arange(slots, dtype=jnp.int32)
    active = ids < term_count[0]
    same = (
        (term_target[:, None] == term_target[None, :])
        & active[None, :]
        & (ids[None, :] < ids[:, None])
    )
    prev = jnp.max(jnp.where(same, ids[None, :], -1), axis=1)
    prev = jnp.where(prev < 0, slots, prev)
    here = (jnp.arange(sectors, dtype=jnp.int32)[:, None] == term_target[None, :]) & active[None, :]
    last = jnp.max(jnp.where(here, ids[None, :], -1), axis=1)
    last = jnp.where(last < 0, slots, last)
    code_rows = per_row * own_cols + 16
    smem = pl.BlockSpec(memory_space=pltpu.SMEM)
    vmem = pl.BlockSpec(memory_space=pltpu.VMEM)
    hbm = pl.BlockSpec(memory_space=pl.ANY)
    dma = pltpu.SemaphoreType.DMA
    return pl.pallas_call(
        functools.partial(kernel, row_total, col_total),
        out_shape=jax.ShapeDtypeStruct((steps, per_row, own_cols, left_size), jnp.float32),
        in_specs=[smem] * 5 + [vmem, hbm, hbm],
        out_specs=vmem,
        scratch_shapes=[
            pltpu.VMEM(left_ops.shape, jnp.bfloat16),
            pltpu.VMEM(right_ops.shape, jnp.bfloat16),
            pltpu.VMEM((col_total, sectors, own_cols, left_size), jnp.bfloat16),
            pltpu.VMEM((2, per_row, own_cols, left_size), jnp.bfloat16),
            pltpu.VMEM((slots + 1, own_cols, left_size), jnp.float32),
            pltpu.VMEM((per_row, own_cols, left_size), jnp.float32),
            pltpu.VMEM((row_total, code_rows, left_size), jnp.int16),
            pltpu.VMEM((row_total + 1, code_rows, left_size), jnp.int16),
            pltpu.VMEM((8, left_size), jnp.float32),
            pltpu.VMEM((peers, 8, left_size), jnp.float32),
            dma((2,)),
            dma((peers,)),
            dma((peers,)),
        ]
        + [dma((row_total + 1,))] * 2
        + [dma((max(pieces, 2 * row_total + 2),))] * 8,
        compiler_params=pltpu.CompilerParams(
            collective_id=0, has_side_effects=True, vmem_limit_bytes=58 * 1024 * 1024
        ),
        cost_estimate=pl.CostEstimate(
            flops=steps * slots * 6 * own_cols * left_size * left_size,
            bytes_accessed=8 * 1024 * 1024,
            transcendentals=0,
        ),
    )(term_source, prev, last, left_dims, right_dims, wavefunction, left_ops, right_ops)


def solution(mesh):
    placed = (
        P("parts", "col", None),
        P(("parts", "row"), None, None),
        P(("parts", "row"), "col", None),
        P(("parts", "row")),
        P(("parts", "row")),
        P(("parts", "row")),
        P("parts"),
        P("parts"),
    )
    return jax.shard_map(
        body,
        mesh=mesh,
        in_specs=placed,
        out_specs=P(None, ("parts", "row"), "col", None),
        check_vma=False,
    )
```

```python
import functools

import jax
import jax.numpy as jnp
from jax import lax
from jax.experimental import pallas as pl
from jax.experimental.pallas import tpu as pltpu
from jax.sharding import PartitionSpec as P

MESH = pl.DeviceIdType.MESH
steps = 3
group = 48
full_code = 32440.0
pieces, shared = 8, 3


def kernel(
    row_total, col_total,
    source_ref, prev_ref, last_ref, left_dim_ref, right_dim_ref,
    wave_ref, left_hbm, right_hbm,
    out_ref,
    left_ref, right_ref, vec, own_vec, accum, total_block, send_code, recv_code, send_sums, recv_sums,
    load_sem, sums_send, sums_recv, code_send, code_recv,
    z_send, z_recv, x_send, x_recv, near_send, near_recv, far_send, far_recv,
):
    sectors, own_cols, left_size = wave_ref.shape
    slots = left_ref.shape[0]
    per_row = sectors // row_total
    block_rows = per_row * own_cols
    halves = 2 if per_row % 2 == 0 else 1
    unroll = 4 if per_row % 4 == 0 else 1
    peers = row_total * col_total
    peer_unroll = 15 if (peers - 1) % 15 == 0 and peers <= 32 else 1
    row = lax.axis_index("row")
    col = lax.axis_index("col")
    flat = row * col_total + col
    x_col = (col + col_total // 2) % col_total
    near_col = col + 1 - 2 * (col % 2)
    cell_total = sectors * own_cols * col_total * left_size

    def peer(n):
        place = (flat + n) % peers
        return {"row": place // col_total, "col": place % col_total}

    loads = [
        pltpu.make_async_copy(left_hbm, left_ref, load_sem.at[0]),
        pltpu.make_async_copy(right_hbm, right_ref, load_sem.at[1]),
    ]
    for load in loads:
        load.start()

    barrier = pltpu.get_barrier_semaphore()

    @pl.loop(1, peers)
    def _(n):
        pl.semaphore_signal(barrier, inc=1, device_id=peer(n), device_id_type=MESH)

    row_ids = lax.broadcasted_iota(jnp.int32, (own_cols, left_size), 0) + col * own_cols
    lane_ids = lax.broadcasted_iota(jnp.int32, (own_cols, left_size), 1)

    def support(s):
        return (row_ids < right_dim_ref[s]) & (lane_ids < left_dim_ref[s])

    @pl.loop(0, sectors, unroll=4)
    def _(s):
        value = wave_ref[s].astype(jnp.float32)
        vec[col, s] = jnp.where(support(s), value, 0.0).astype(jnp.bfloat16)

    @pl.loop(0, per_row)
    def _(j):
        own_vec[0, j] = vec[col, row * per_row + j]

    accum[slots] = jnp.zeros((own_cols, left_size), jnp.float32)
    pl.semaphore_wait(barrier, peers - 1)

    def move(which, start, size, send, recv, row_to, col_to):
        ref = vec.at[which, pl.ds(start, size)]
        return pltpu.make_async_remote_copy(
            src_ref=ref, dst_ref=ref, send_sem=send, recv_sem=recv,
            device_id={"row": row_to, "col": col_to}, device_id_type=MESH,
        )

    def mirror(r):
        return jnp.where(row < 2, r, 3 - r)

    def spread_first():
        size = sectors // pieces
        side = row % 2
        alone = [side * shared + i for i in range(shared)]
        other = [(1 - side) * shared + i for i in range(shared)]
        common = list(range(2 * shared, pieces))

        def x_move(k):
            return move(col, k * size, size, x_send.at[k], x_recv.at[k], row, x_col)

        def pair_move(k):
            return move(
                x_col, k * size, size, z_send.at[k], z_recv.at[k], row + 1 - 2 * side, col
            )

        def near_move():
            return move(col, 0, sectors, near_send.at[0], near_recv.at[0], row, near_col)

        def far_move(k):
            return move(x_col, k * size, size, far_send.at[k], far_recv.at[k], row, near_col)

        for k in alone + common:
            x_move(k).start()
        near_move().start()
        for k in alone:
            x_move(k).wait_recv()
            pair_move(k).start()
            far_move(k).start()
        for mine, theirs in zip(common + [None] * shared, other):
            if mine is not None:
                x_move(mine).wait_recv()
                far_move(mine).start()
            pair_move(theirs).wait_recv()
            far_move(theirs).start()
        for k in alone + common:
            x_move(k).wait_send()
        for k in alone:
            pair_move(k).wait_send()
        near_move().wait()

        @pl.loop(0, pieces)
        def _(k):
            far_move(k).wait()

    def spread():
        size = per_row // halves

        def part(which, b, h, send, recv, k, row_to, col_to):
            return move(
                which, b * per_row + h * size, size, send.at[k * halves + h],
                recv.at[b * halves + h], row_to, col_to,
            )

        def z_move(to, h):
            return part(col, row, h, z_send, z_recv, to, to, col)

        def z_arrival(b, h):
            return part(col, b, h, z_send, z_recv, b, row, near_col)

        def relay_move(h):
            return part(col, mirror(2), h, z_send, z_recv, row_total, mirror(0), col)

        def x_move(b, h):
            return part(col, b, h, x_send, x_recv, b, row, x_col)

        def near_move(b, h):
            return part(col, b, h, near_send, near_recv, b, row, near_col)

        def far_move(b, h):
            return part(x_col, b, h, far_send, far_recv, b, row, near_col)

        def start_all(b, h):
            x_move(b, h).start()
            near_move(b, h).start()

        def arrived(b, relay=False):
            for h in range(halves):
                z_arrival(b, h).wait_recv()
                if relay:
                    @pl.when(middle)
                    def _():
                        relay_move(h).start()
                start_all(b, h)

        def x_arrived(b):
            for h in range(halves):
                x_move(b, h).wait_recv()
                far_move(b, h).start()

        for h in range(halves):
            x_move(row, h).start()
        if row_total == 4:
            middle = (row == 1) | (row == 2)
            inner = middle.astype(jnp.int32)
            order = [mirror(1 + inner), mirror(3 - 3 * inner), mirror(2 + inner)]
            sends = [mirror(3 - inner), mirror(2 - 2 * inner)]
            for to in sends:
                for h in range(halves):
                    z_move(to, h).start()

            @pl.when(jnp.logical_not(middle))
            def _():
                for h in range(halves):
                    z_move(mirror(1), h).start()

            for h in range(halves):
                near_move(row, h).start()
            arrived(order[0], True)
            x_arrived(row)
            arrived(order[1])
            x_arrived(order[0])
            arrived(order[2])
            x_arrived(order[1])
            x_arrived(order[2])
            for h in range(halves):
                for to in sends:
                    z_move(to, h).wait_send()

                @pl.when(jnp.logical_not(middle))
                def _():
                    z_move(mirror(1), h).wait_send()

                @pl.when(middle)
                def _():
                    relay_move(h).wait_send()
        else:
            @pl.loop(1, row_total)
            def _(d):
                for h in range(halves):
                    z_move((row + d) % row_total, h).start()

            for h in range(halves):
                near_move(row, h).start()

            @pl.loop(1, row_total)
            def _(d):
                arrived((row + row_total - d) % row_total)

            @pl.loop(0, row_total)
            def _(b):
                x_arrived(b)

            @pl.loop(1, row_total)
            def _(d):
                for h in range(halves):
                    z_move((row + d) % row_total, h).wait_send()

        @pl.loop(0, row_total, unroll=unroll)
        def _(b):
            for h in range(halves):
                near_move(b, h).wait()
                far_move(b, h).wait()
                x_move(b, h).wait_send()

    def apply_terms():
        @pl.loop(0, slots // group)
        def _(g):
            outs = []
            for i in range(group):
                p = g * group + i
                block = vec[:, source_ref[p]].reshape(col_total * own_cols, left_size)
                part = jnp.dot(right_ref[p], block, preferred_element_type=jnp.float32)
                high = part.astype(jnp.bfloat16)
                low = (part - high.astype(jnp.float32)).astype(jnp.bfloat16)
                both = jnp.dot(
                    jnp.concatenate([high, low], axis=0), left_ref[p],
                    preferred_element_type=jnp.float32,
                )
                outs.append(both[:own_cols] + both[own_cols:])
            for i in range(group):
                p = g * group + i
                accum[p] = outs[i] + accum[prev_ref[p]]

    def code_move(o, slot, row_to):
        return pltpu.make_async_remote_copy(
            src_ref=send_code.at[o], dst_ref=recv_code.at[slot],
            send_sem=code_send.at[o], recv_sem=code_recv.at[slot],
            device_id={"row": row_to, "col": col}, device_id_type=MESH,
        )

    def sums_move(n):
        return pltpu.make_async_remote_copy(
            src_ref=send_sums, dst_ref=recv_sums.at[n],
            send_sem=sums_send.at[n], recv_sem=sums_recv.at[n],
            device_id=peer(n), device_id_type=MESH,
        )

    def scale_of(slot):
        level = recv_code[slot, pl.ds(block_rows, 16)].astype(jnp.int32).astype(jnp.float32)
        return jnp.exp2(level[0:1, :]) * (1.0 / full_code)

    def rows_of(j):
        return pl.ds(pl.multiple_of(j * own_cols, 16), own_cols)

    def decode(slot, j, scale):
        return recv_code[slot, rows_of(j)].astype(jnp.int32).astype(jnp.float32) * scale

    def relay(o, slot, first):
        scale = None if first else scale_of(slot)

        def gather(j, top):
            value = accum[last_ref[o * per_row + j]]
            if not first:
                value = value + decode(slot, j, scale)
            total_block[j] = value
            return jnp.maximum(top, jnp.abs(value))

        top = lax.fori_loop(
            0, per_row, gather, jnp.full((own_cols, left_size), 1e-30, jnp.float32),
            unroll=unroll,
        )
        level = jnp.ceil(jnp.log2(jnp.max(top, axis=(0, 1), keepdims=True)))
        factor = jnp.exp2(-level) * full_code
        send_code[o, pl.ds(block_rows, 16)] = (
            jnp.broadcast_to(level, (16, left_size)).astype(jnp.int32).astype(jnp.int16)
        )

        @pl.loop(0, per_row, unroll=unroll)
        def _(j):
            value = jnp.round(total_block[j] * factor)
            send_code[o, rows_of(j)] = value.astype(jnp.int32).astype(jnp.int16)

    def reduce_partials(step):
        def send(o):
            relay(o, 0, True)
            code_move(o, row, o).start()

        def receive(r):
            code_move(row, r, near_row).wait_recv()
            scale = scale_of(r)

            @pl.loop(0, per_row, unroll=unroll)
            def _(j):
                out_ref[step, j] += decode(r, j, scale)

        near_row = (row + 1) % row_total

        def take_own():
            @pl.loop(0, per_row, unroll=unroll)
            def _(j):
                out_ref[step, j] = accum[last_ref[row * per_row + j]]

        if row_total == 4:
            middle = (row == 1) | (row == 2)
            end = jnp.logical_not(middle)

            @pl.when(end)
            def _():
                relay(mirror(3), 0, True)
                code_move(mirror(3), row_total, mirror(1)).start()
                send(mirror(2))
                send(mirror(1))

            @pl.when(middle)
            def _():
                send(mirror(2))
                send(mirror(0))
                code_move(row, row_total, near_row).wait_recv()
                relay(mirror(3), row_total, False)
                code_move(mirror(3), row, mirror(3)).start()

            take_own()

            @pl.when(end)
            def _():
                receive(mirror(1))
                receive(mirror(2))

            @pl.when(middle)
            def _():
                receive(mirror(2))
                receive(mirror(0))
                receive(mirror(3))
        else:
            @pl.loop(1, row_total)
            def _(d):
                send((row + d) % row_total)

            take_own()

            @pl.loop(1, row_total)
            def _(d):
                receive((row + row_total - d) % row_total)

        @pl.loop(0, per_row, unroll=unroll)
        def _(j):
            out_ref[step, j] = jnp.where(support(row * per_row + j), out_ref[step, j], 0.0)

        @pl.loop(1, row_total)
        def _(d):
            o = (row + d) % row_total
            code_move(o, row, near_row).wait_send()

    def fold(value):
        return jnp.sum(value, axis=0, keepdims=True)

    spread_first()
    for load in loads:
        load.wait()
    grams = {}
    for step in range(steps):
        apply_terms()
        reduce_partials(step)

        if step + 1 == steps:
            break
        pairs = [(i, step) for i in range(step + 1)]
        count = 1 + (step + 1) + len(pairs)

        def add_sums(j, totals):
            sigma = out_ref[step, j]
            wide = [own_vec[i, j].astype(jnp.float32) for i in range(step + 1)]
            items = [sigma * sigma] + [entry * sigma for entry in wide]
            items += [wide[i] * wide[k] for i, k in pairs]
            return tuple(a + b for a, b in zip(totals, items))

        zero = jnp.zeros((own_cols, left_size), jnp.float32)
        totals = lax.fori_loop(0, per_row, add_sums, (zero,) * count, unroll=unroll)
        rows = [fold(total) for total in totals]
        rows += [jnp.zeros((8 - count, left_size), jnp.float32)]
        send_sums[...] = jnp.concatenate(rows, axis=0)

        @pl.loop(1, peers, unroll=peer_unroll)
        def _(n):
            sums_move(n).start()

        def gather_sums(n, total):
            sums_move(n).wait()
            return total + recv_sums[n]

        total = lax.fori_loop(1, peers, gather_sums, send_sums[...], unroll=peer_unroll)
        total = jnp.sum(total, axis=1, keepdims=True)
        values = [total[i : i + 1] for i in range(count)]
        square, correlations = values[0], values[1 : step + 2]
        for pair, value in zip(pairs, values[step + 2 :]):
            grams[pair] = value
        weights = [
            correlations[i] / (grams[(i, i)] + 1e-06) for i in range(step + 1)
        ]
        for i in range(step + 1):
            square = square - 2.0 * weights[i] * correlations[i]
            for k in range(step + 1):
                square = square + weights[i] * weights[k] * grams[(min(i, k), max(i, k))]
        mean_sq = jnp.maximum(square, 0.0) / cell_total
        factor = lax.rsqrt(mean_sq + 1e-06)

        @pl.loop(0, per_row)
        def _(j):
            remainder = out_ref[step, j]
            for i in range(step + 1):
                remainder = remainder - weights[i] * own_vec[i, j].astype(jnp.float32)
            fresh = (remainder * factor).astype(jnp.bfloat16)
            vec[col, row * per_row + j] = fresh
            if step + 2 < steps:
                own_vec[step + 1, j] = fresh

        spread()


def body(
    wavefunction, left_ops, right_ops, term_source, term_target, term_count, left_dims, right_dims
):
    row_total = lax.axis_size("row")
    col_total = lax.axis_size("col")
    peers = row_total * col_total
    sectors, own_cols, left_size = wavefunction.shape
    slots = left_ops.shape[0]
    per_row = sectors // row_total
    ids = jnp.arange(slots, dtype=jnp.int32)
    active = ids < term_count[0]
    same = (
        (term_target[:, None] == term_target[None, :])
        & active[None, :]
        & (ids[None, :] < ids[:, None])
    )
    prev = jnp.max(jnp.where(same, ids[None, :], -1), axis=1)
    prev = jnp.where(prev < 0, slots, prev)
    here = (jnp.arange(sectors, dtype=jnp.int32)[:, None] == term_target[None, :]) & active[None, :]
    last = jnp.max(jnp.where(here, ids[None, :], -1), axis=1)
    last = jnp.where(last < 0, slots, last)
    code_rows = per_row * own_cols + 16
    smem = pl.BlockSpec(memory_space=pltpu.SMEM)
    vmem = pl.BlockSpec(memory_space=pltpu.VMEM)
    hbm = pl.BlockSpec(memory_space=pl.ANY)
    dma = pltpu.SemaphoreType.DMA
    return pl.pallas_call(
        functools.partial(kernel, row_total, col_total),
        out_shape=jax.ShapeDtypeStruct((steps, per_row, own_cols, left_size), jnp.float32),
        in_specs=[smem] * 5 + [vmem, hbm, hbm],
        out_specs=vmem,
        scratch_shapes=[
            pltpu.VMEM(left_ops.shape, jnp.bfloat16),
            pltpu.VMEM(right_ops.shape, jnp.bfloat16),
            pltpu.VMEM((col_total, sectors, own_cols, left_size), jnp.bfloat16),
            pltpu.VMEM((2, per_row, own_cols, left_size), jnp.bfloat16),
            pltpu.VMEM((slots + 1, own_cols, left_size), jnp.float32),
            pltpu.VMEM((per_row, own_cols, left_size), jnp.float32),
            pltpu.VMEM((row_total, code_rows, left_size), jnp.int16),
            pltpu.VMEM((row_total + 1, code_rows, left_size), jnp.int16),
            pltpu.VMEM((8, left_size), jnp.float32),
            pltpu.VMEM((peers, 8, left_size), jnp.float32),
            dma((2,)),
            dma((peers,)),
            dma((peers,)),
        ]
        + [dma((row_total + 1,))] * 2
        + [dma((max(pieces, 2 * row_total + 2),))] * 8,
        compiler_params=pltpu.CompilerParams(
            collective_id=0, has_side_effects=True, vmem_limit_bytes=58 * 1024 * 1024
        ),
        cost_estimate=pl.CostEstimate(
            flops=steps * slots * 6 * own_cols * left_size * left_size,
            bytes_accessed=8 * 1024 * 1024,
            transcendentals=0,
        ),
    )(term_source, prev, last, left_dims, right_dims, wavefunction, left_ops, right_ops)


def solution(mesh):
    placed = (
        P("parts", "col", None),
        P(("parts", "row"), None, None),
        P(("parts", "row"), "col", None),
        P(("parts", "row")),
        P(("parts", "row")),
        P(("parts", "row")),
        P("parts"),
        P("parts"),
    )
    return jax.shard_map(
        body,
        mesh=mesh,
        in_specs=placed,
        out_specs=P(None, ("parts", "row"), "col", None),
        check_vma=False,
    )
```
